256 devices in a mesh: occ: 8 (over y, x_lo), cabs: 16 (over z, core), aux: 2 (over x_hi).
Axes of the slice: x: 4 (x_hi: 2, x_lo: 2; x = x_hi * 2 + x_lo), y: 4, z: 8, core: 2. Of those that a mesh axis runs over, the one named last changes fastest.
Arguments:
- occ_fit: bfloat16 [8, 160, 5120], P('occ', None, 'aux'), may hold values from -6 to 6
- cabs_fit: bfloat16 [8, 4096, 5120], P('occ', 'cabs', 'aux'), may hold values from -0.0034179688 to 0.0034179688
- fock: bfloat16 [4096, 4096], P(None, 'cabs'), may hold values from -1.5 to 1.5, as said below
- cabs_block: int32 [4096], replicated, may hold values from 0 to 1
- pair_block: int32 [8], replicated, may hold values from 0 to 1
Outputs:
- pair_exchange: float32 [8, 8], P('occ')
The draws below stay inside these ranges and needn't reach their ends.
Inputs may be any that keep to these rules, and one draw needn't show every extreme that they name: fock is symmetric.
All inputs are finite; a program needn't handle non-finite values.
Results may differ from the reference program's by a relative error of at most 0.0028.
Values may be sent and summed in bfloat16 or wider, within the bound.
No kernel may reach another device: no remote copies, remote signals or barrier semaphores. Data moves between devices by JAX's collectives and lax.ppermute only.
A program may use at most 64 MiB of HBM per device.

```python
import math
import jax
import jax.numpy as jnp

CABS = 4096
FIT = 5120
M_OCC = 160
NOCC = 8


def draw_fock(key, part):
    key = jax.random.fold_in(key, 11)
    key_rough, key_diag = jax.random.split(key)
    rough = jax.random.normal(key_rough, (CABS, CABS), jnp.float32)
    diagonal = jax.random.uniform(key_diag, (CABS,), jnp.float32, -1.0, 1.0)
    rough = jnp.clip(rough, -4.0, 4.0)
    matrix = (rough + rough.T) * (0.5 / math.sqrt(CABS)) + jnp.diag(diagonal)
    return matrix.astype(jnp.bfloat16)


def with_ends(array, key, low, high):
    shape = array.shape
    index_at = [jax.random.randint(jax.random.fold_in(key, axis), (), 0, shape[axis]) for axis in range(len(shape))]
    array = array.at[tuple(index_at)].set(low)
    longest = shape.index(max(shape))
    index_at[longest] = (index_at[longest] + 1) % shape[longest]
    return array.at[tuple(index_at)].set(high)


def levels(key, dims, cuts, least, largest):
    def one(position, parts):
        draws = jax.random.uniform(jax.random.fold_in(jax.random.fold_in(key, 6), position), (parts,), jnp.float32, least / len(cuts), largest / len(cuts))
        return jnp.repeat(jnp.exp(draws), dims[position] // parts).reshape((-1,) + (1,) * (len(dims) - position - 1))

    level = one(*cuts[0])
    for cut in cuts[1:]:
        level = level * one(*cut)
    return level


def gaussian(rng, extent, scale, reach, cuts=(), dtype=jnp.bfloat16):
    level = levels(rng, extent, cuts, -0.22, 0.18) if cuts else 1.0
    entries = jax.random.normal(rng, extent, jnp.float32) * scale * level
    return jnp.minimum(jnp.maximum(entries, -reach), reach).astype(dtype)


def setup_inputs(seed: int = 0) -> dict:
    splits = jax.random.split(jax.random.key(seed), 6)
    return {
        "occ_fit": gaussian(splits[0], (NOCC, M_OCC, FIT), 1.0, 6.0, ((0, 8), (2, 2))),
        "cabs_fit": gaussian(splits[1], (NOCC, CABS, FIT), (4 * FIT * M_OCC) ** -0.5, 0.0034179688, ((0, 8), (1, 16), (2, 2))),
        "fock": draw_fock(jax.random.fold_in(splits[5], 71), 0),
        "cabs_block": with_ends(jax.random.randint(splits[3], (CABS,), 0, 2), jax.random.fold_in(splits[3], 1), 0, 1).astype(jnp.int32),
        "pair_block": with_ends(jax.random.randint(splits[4], (NOCC,), 0, 2), jax.random.fold_in(splits[4], 1), 0, 1).astype(jnp.int32),
    }


def reference(occ_fit, cabs_fit, fock, cabs_block, pair_block):
    left_rows = occ_fit.reshape(NOCC * M_OCC, FIT)
    right_rows = cabs_fit.reshape(NOCC * CABS, FIT)
    direct = jnp.dot(left_rows, right_rows.T, preferred_element_type=jnp.float32)
    direct = direct.reshape(NOCC, M_OCC, NOCC, CABS).transpose(0, 2, 1, 3).astype(jnp.bfloat16)
    swapped = direct.transpose(1, 0, 2, 3)
    same_block = cabs_block[:, None] == cabs_block[None, :]
    coupled = jnp.where(same_block, fock, jnp.zeros_like(fock))
    applied = jnp.dot(swapped.reshape(NOCC * NOCC * M_OCC, CABS), coupled, preferred_element_type=jnp.float32)
    applied = applied.reshape(NOCC, NOCC, M_OCC, CABS)
    pair_label = (pair_block[:, None] + pair_block[None, :]) % 2
    per_column = jnp.sum(direct.astype(jnp.float32) * applied, axis=2)
    keep_column = cabs_block[None, None, :] == pair_label[:, :, None]
    return jnp.sum(jnp.where(keep_column, per_column, jnp.float32(0.0)), axis=2)
```

```python
import jax
import jax.numpy as jnp
from jax import lax
from jax.sharding import PartitionSpec as P

BF = jnp.bfloat16
F32 = jnp.float32
Y = 4
Z = 8


def occ_hop(value, dy, flip):
    pairs = []
    for o in range(2 * Y):
        y, xl = o // 2, o % 2
        pairs.append((o, ((y + dy) % Y) * 2 + (xl ^ flip)))
    return lax.ppermute(value, "occ", pairs)


def z_hop(value, dz):
    return lax.ppermute(value, "cabs", [(c, ((c // 2 + dz) % Z) * 2 + c % 2) for c in range(2 * Z)])


def core_swap(value):
    return lax.ppermute(value, "cabs", [(c, c ^ 1) for c in range(2 * Z)])


def aux_swap(value):
    return lax.ppermute(value, "aux", [(0, 1), (1, 0)])


def rows_dot(left, right):
    return lax.dot_general(left, right, (((1,), (1,)), ((), ())), preferred_element_type=F32)


def plain_dot(left, right):
    return lax.dot_general(left, right, (((1,), (0,)), ((), ())), preferred_element_type=F32)


def shards(occ_fit, cabs_fit, fock, cabs_block, pair_block):
    me = lax.axis_index("occ")
    cabs = lax.axis_index("cabs")
    side = lax.axis_index("aux")
    core = cabs % 2
    z = cabs // 2
    my_y, my_x = me // 2, me % 2
    m_rows, fit = occ_fit.shape[1:]
    width = cabs_fit.shape[1]
    half_fit = fit // 2
    half = m_rows // 2
    quarter = half // 2

    mine = lax.dynamic_slice_in_dim(occ_fit[0], core * half_fit, half_fit, 1)
    own = jnp.where(side == 0, mine, jnp.concatenate([mine[half:], mine[:half]], 0))
    slab = cabs_fit[0]
    slab_own = lax.dynamic_slice_in_dim(slab, core * half_fit, half_fit, 1)
    slab_other = lax.dynamic_slice_in_dim(slab, (1 - core) * half_fit, half_fit, 1)

    by_core = fock.reshape(Z, 2, width, width)
    tile_own = lax.dynamic_index_in_dim(by_core, core, 1, False)
    tile_send = lax.dynamic_index_in_dim(by_core, 1 - core, 1, False)
    tile_other = core_swap(tile_send)

    p0 = occ_hop(own, 0, 1)
    a = occ_hop(own, 1, 0)
    b = occ_hop(own, -1, 0)
    pb = occ_hop(b, 0, 1)
    pa = occ_hop(p0, 1, 0)
    c = occ_hop(b, -1, 0)
    cut1, cut2 = 48, 96
    pc = jnp.concatenate(
        [occ_hop(pa[:cut1], 1, 0), occ_hop(pb[cut1:cut2], -1, 0), occ_hop(c[cut2:], 0, 1)], 0
    )

    labels = lax.dynamic_slice_in_dim(cabs_block, cabs * width, width)

    def partner(dy, flip):
        return ((my_y + dy) % Y) * 2 + (my_x + flip) % 2

    def label_of(dy, flip):
        return (pair_block[me] + pair_block[partner(dy, flip)]) % 2

    def integrals(slices, places):
        keep, send = [], []
        for part in slices:
            other = core_swap(part)
            total = rows_dot(part, slab_own) + rows_dot(other, slab_other)
            keep.append(total[:half])
            send.append(total[half:])
        got = aux_swap(jnp.stack(send))
        whole = (jnp.stack(keep) + got).astype(BF)
        want = jnp.stack([label_of(dy, flip) for dy, flip in places])
        return jnp.where(labels[None, None, :] == want[:, None, None], whole, jnp.zeros_like(whole))

    d_self, d_p0, d_a, d_b = integrals([own, p0, a, b], [(0, 0), (0, 1), (-1, 0), (1, 0)])
    d_pb, d_pa, d_c = integrals([pb, pa, c], [(1, 1), (-1, 1), (2, 0)])
    (d_pc,) = integrals([pc], [(2, 1)])

    def halves(value, second):
        take = lax.dynamic_slice_in_dim(value, jnp.where(second, quarter, 0), quarter, 0)
        give = lax.dynamic_slice_in_dim(value, jnp.where(second, 0, quarter), quarter, 0)
        return take, give

    high_x = my_x == 1
    high_y = my_y >= 2
    take_p0, give_p0 = halves(d_p0, high_x)
    take_c, give_c = halves(d_c, high_y)
    take_pc, give_pc = halves(d_pc, high_y)

    left = jnp.concatenate([d_self, d_a, take_p0, d_pa, take_c, take_pc], 0)
    right = jnp.concatenate(
        [
            d_self,
            occ_hop(d_b, 1, 0),
            occ_hop(give_p0, 0, 1),
            occ_hop(d_pb, 1, 1),
            occ_hop(give_c, 2, 0),
            occ_hop(give_pc, 2, 1),
        ],
        0,
    )
    right_other = core_swap(right)

    rows = left.shape[0]
    cut = (rows // 2 + 15) // 16 * 16
    blocks = [(0, left)]
    up = down = left
    for step in range(1, Z // 2):
        up, down = z_hop(up, 1), z_hop(down, -1)
        blocks += [(-step, up), (step, down)]
    blocks.append((Z // 2, jnp.concatenate([z_hop(up[:cut], 1), z_hop(down[cut:], -1)], 0)))
    applied_own = applied_other = 0.0
    for offset, block in blocks:
        place = (z + offset) % Z
        applied_own += plain_dot(block, lax.dynamic_index_in_dim(tile_own, place, 0, False))
        applied_other += plain_dot(block, lax.dynamic_index_in_dim(tile_other, place, 0, False))
    product = applied_own * right.astype(F32) + applied_other * right_other.astype(F32)
    per_row = jnp.sum(product, axis=1)
    spans = [half, half, quarter, half, quarter, quarter]
    sums, start = [], 0
    for span in spans:
        sums.append(jnp.sum(per_row[start : start + span]))
        start += span
    s_self, s_a, s_p0, s_pa, s_c, s_pc = sums
    g_b = occ_hop(s_a, -1, 0)
    g_pb = occ_hop(s_pa, -1, 1)
    g_p0 = occ_hop(s_p0, 0, 1)
    g_c = occ_hop(s_c, 2, 0)
    g_pc = occ_hop(s_pc, 2, 1)
    places = [(0, 0), (0, 1), (1, 0), (1, 1), (2, 0), (2, 1), (-1, 0), (-1, 1)]
    values = [s_self, s_p0 + g_p0, g_b, g_pb, s_c + g_c, s_pc + g_pc, s_a, s_pa]
    row = jnp.zeros((2 * Y,), F32)
    lane = lax.iota(jnp.int32, 2 * Y)
    for (dy, flip), value in zip(places, values):
        row += jnp.where(lane == partner(dy, flip), value, jnp.float32(0.0))
    peers = 4 * Z
    spread = lax.all_to_all(
        jnp.broadcast_to(row, (peers, 2 * Y)), ("cabs", "aux"), 0, 0, tiled=True
    )
    return jnp.sum(spread, axis=0)[None, :]


def solution(mesh):
    in_specs = (P("occ", None, "aux"), P("occ", "cabs", "aux"), P(None, "cabs"), P(), P())
    out_specs = P("occ", None)
    return jax.shard_map(shards, mesh=mesh, in_specs=in_specs, out_specs=out_specs, check_vma=False)
```

```python
import jax
import jax.numpy as jnp
from jax import lax
from jax.experimental import pallas as pl
from jax.experimental.pallas import tpu as pltpu
from jax.sharding import PartitionSpec as P

BF = jnp.bfloat16
F32 = jnp.float32
Y = 4
Z = 8
OCC = 2 * Y
KEPT = 40
HEAD = 48
VMEM = pl.BlockSpec(memory_space=pltpu.VMEM)
SMEM = pl.BlockSpec(memory_space=pltpu.SMEM)
ANY = pl.BlockSpec(memory_space=pl.ANY)
PARAMS = pltpu.CompilerParams(vmem_limit_bytes=12 * 2**20)

PLACES = ((0, 0), (0, 1), (-1, 0), (1, 0), (1, 1), (-1, 1), (2, 0), (2, 1))


def partner(me, dy, flip):
    return (((me >> 1) + dy) & (Y - 1)) * 2 + ((me & 1) ^ flip)


def occ_hop(value, dy, flip):
    return lax.ppermute(value, "occ", [(o, partner(o, dy, flip)) for o in range(OCC)])


def px_hop(value, flips):
    pairs = []
    for o in range(OCC):
        takes_c = (o & 1) ^ (o >> 2)
        pairs.append((o, partner(o, 0, 1) if takes_c == flips else partner(o, 2, 0)))
    return lax.ppermute(value, "occ", pairs)


def z_hop(value, dz):
    return lax.ppermute(value, "cabs", [(c, ((c // 2 + dz) % Z) * 2 + c % 2) for c in range(2 * Z)])


def core_swap(value):
    return lax.ppermute(value, "cabs", [(c, c ^ 1) for c in range(2 * Z)])


def aux_swap(value):
    return lax.ppermute(value, "aux", [(0, 1), (1, 0)])


def rows_dot(left, right):
    return lax.dot_general(left, right, (((1,), (1,)), ((), ())), preferred_element_type=F32)


def plain_dot(left, right):
    return lax.dot_general(left, right, (((1,), (0,)), ((), ())), preferred_element_type=F32)


def transposed(slab, slab_other):
    width, fit = slab.shape

    def body(own_ref, other_ref, out_ref):
        out_ref[:, :width] = own_ref[...].T
        out_ref[:, width:] = other_ref[...].T

    return pl.pallas_call(
        body,
        out_shape=jax.ShapeDtypeStruct((fit, 2 * width), BF),
        in_specs=[VMEM, VMEM],
        out_specs=VMEM,
        compiler_params=PARAMS,
        cost_estimate=pl.CostEstimate(
            flops=0, bytes_accessed=8 * fit * width, transcendentals=0
        ),
    )(slab, slab_other)


def fit_sums(place, slices, columns, kept_before=None):
    count = len(slices)
    rows, fit = slices[0].shape
    width = columns.shape[1]
    extra = [] if kept_before is None else [kept_before]
    shapes = [jax.ShapeDtypeStruct((count, KEPT, width), F32)]
    if not extra:
        shapes.append(jax.ShapeDtypeStruct((count, KEPT, width), F32))

    def body(place_ref, *refs):
        parts, columns_ref = refs[:count], refs[count]
        stack_ref, total_ref, sems = refs[-3:]
        outs = refs[count + 1 + len(extra) : -3]
        copies = [
            pltpu.make_async_copy(
                parts[index], stack_ref.at[pl.ds(index * rows, rows), :], sems.at[index]
            )
            for index in range(count)
        ]
        for copy in copies:
            copy.start()
        for copy in copies:
            copy.wait()
        total_ref[...] = plain_dot(stack_ref[...], columns_ref[...])
        side = place_ref[3]
        for index in range(count):
            start = index * rows

            def taken(first, length):
                return total_ref[pl.ds(pl.multiple_of(start + first, 8), length), :]

            if rows == 2 * KEPT:
                outs[0][index] = taken(side * KEPT, KEPT)
                outs[1][index] = taken((1 - side) * KEPT, KEPT)
            elif not extra:
                over = rows - KEPT
                outs[0][index, :over, :] = taken(side * KEPT, over)
                outs[1][index] = taken((1 - side) * over, KEPT)
            else:
                over = KEPT - rows
                few = refs[count + 1][index, :over, :]
                outs[0][index, pl.ds(pl.multiple_of(side * over, 8), rows), :] = taken(0, rows)
                outs[0][index, pl.ds(pl.multiple_of((1 - side) * rows, 8), over), :] = few

    return pl.pallas_call(
        body,
        out_shape=tuple(shapes),
        in_specs=[SMEM] + [ANY] * count + [VMEM] * (1 + len(extra)),
        out_specs=(VMEM,) * len(shapes),
        scratch_shapes=[
            pltpu.VMEM((count * rows, fit), BF),
            pltpu.VMEM((count * rows, width), F32),
            pltpu.SemaphoreType.DMA((count,)),
        ],
        compiler_params=PARAMS,
        cost_estimate=pl.CostEstimate(
            flops=2 * count * rows * fit * width,
            bytes_accessed=2 * width * fit + 2 * count * rows * fit + 8 * count * rows * width,
            transcendentals=0,
        ),
    )(place, *slices, columns, *extra)


def apply_tile(place_ref, offset, block, own_ref, other_ref):
    width = own_ref.shape[1]
    own = other = None
    for index in range(2):
        row = (((place_ref[1] + offset) & (Z - 1)) * 2 + (place_ref[2] ^ index)) * width
        rows = pl.ds(pl.multiple_of(row, width), width)
        part = block[:, index * width : (index + 1) * width]
        to_own = plain_dot(part, own_ref[rows, :])
        to_other = plain_dot(part, other_ref[rows, :])
        own = to_own if own is None else own + to_own
        other = to_other if other is None else other + to_other
    return own, other


def apply_near(place, offsets, blocks, fock, fock_other):
    count = len(blocks)
    rows, columns = blocks[0].shape
    width = columns // 2

    def body(place_ref, *refs):
        own_ref, other_ref, out_ref = refs[count:]
        for index in range(count):
            own, other = apply_tile(
                place_ref, offsets[index], refs[index][...], own_ref, other_ref
            )
            if index == 0:
                out_ref[:, :width] = own
                out_ref[:, width:] = other
            else:
                out_ref[:, :width] += own
                out_ref[:, width:] += other

    return pl.pallas_call(
        body,
        out_shape=jax.ShapeDtypeStruct((rows, columns), F32),
        in_specs=[SMEM] + [VMEM] * (count + 2),
        out_specs=VMEM,
        compiler_params=PARAMS,
        cost_estimate=pl.CostEstimate(
            flops=2 * count * rows * columns * columns,
            bytes_accessed=2 * count * columns * (rows + columns),
            transcendentals=0,
        ),
    )(place, *blocks, fock, fock_other)


def apply_last(place, applied, upper, lower, fock, fock_other, rights):
    cut = upper.shape[0]
    rows, columns = applied.shape
    width = columns // 2
    count = len(rights)
    span = rows // count

    def body(place_ref, applied_ref, upper_ref, lower_ref, own_ref, other_ref, *refs):
        right_refs, (row_ref, a_ref, pa_ref, px_ref, sum_ref) = refs[:count], refs[count:]
        for part, first, last in ((upper_ref, 0, cut), (lower_ref, cut, rows)):
            own, other = apply_tile(place_ref, Z // 2, part[...], own_ref, other_ref)
            sum_ref[first:last, :width] = applied_ref[first:last, :width] + own
            sum_ref[first:last, width:] = applied_ref[first:last, width:] + other
        sums = []
        for index in range(count):
            product = sum_ref[index * span : (index + 1) * span, :] * right_refs[index][...].astype(F32)
            sums.append(jnp.sum(jnp.sum(product, axis=0, keepdims=True), axis=1, keepdims=True))
        me = place_ref[0]
        takes_c = (me & 1) ^ (me >> 2)
        lanes = lax.broadcasted_iota(jnp.int32, (1, OCC), 1)
        px = jnp.where(takes_c == 1, partner(me, 2, 0), partner(me, 0, 1))
        others = (me, partner(me, -1, 0), partner(me, -1, 1), px, partner(me, 2, 1))
        row = jnp.zeros((1, OCC), F32)
        for value, place_of in zip(sums, others):
            row += jnp.where(lanes == place_of, value, 0.0)
        row_ref[...] = row
        here = lanes == me
        a_ref[...] = jnp.where(here, sums[1], 0.0)
        pa_ref[...] = jnp.where(here, sums[2], 0.0)
        px_ref[...] = jnp.where(here, sums[3], 0.0)

    shape = jax.ShapeDtypeStruct((1, OCC), F32)
    return pl.pallas_call(
        body,
        out_shape=(shape,) * 4,
        in_specs=[SMEM] + [VMEM] * (count + 5),
        out_specs=(VMEM,) * 4,
        scratch_shapes=[pltpu.VMEM((rows, columns), F32)],
        compiler_params=PARAMS,
        cost_estimate=pl.CostEstimate(
            flops=2 * rows * columns * columns,
            bytes_accessed=2 * columns * (rows + columns) + 6 * rows * columns,
            transcendentals=0,
        ),
    )(place, applied, upper, lower, fock, fock_other, *rights)


def shards(occ_fit, cabs_fit, fock, cabs_block, pair_block):
    me = lax.axis_index("occ")
    cabs = lax.axis_index("cabs")
    side = lax.axis_index("aux")
    core = cabs & 1
    z = cabs >> 1
    place = jnp.stack([me, z, core, side]).astype(jnp.int32)
    m_rows = occ_fit.shape[1]
    width = cabs_fit.shape[1]
    half = m_rows // 2

    own = lax.dynamic_slice_in_dim(occ_fit[0], core * half, half, 0)
    slab_other = core_swap(cabs_fit[0])
    fock_other = core_swap(fock)

    dy = jnp.array([p[0] for p in PLACES], jnp.int32)
    flip = jnp.array([p[1] for p in PLACES], jnp.int32)
    onehot = partner(me, dy, flip)[:, None] == lax.iota(jnp.int32, OCC)[None, :]
    theirs = jnp.sum(jnp.where(onehot, pair_block[None, :], 0), axis=1)
    mine = jnp.sum(jnp.where(lax.iota(jnp.int32, OCC) == me, pair_block, 0))
    wanted = (theirs + mine) & 1
    by_core = cabs_block.reshape(Z, 2, width)
    chip_labels = jnp.sum(
        jnp.where(lax.iota(jnp.int32, Z)[:, None, None] == z, by_core, 0), axis=0
    )
    labels = jnp.where(core == 0, chip_labels, chip_labels[::-1]).reshape(2 * width)
    keep_column = labels[None] == wanted[:, None]

    p0 = occ_hop(own, 0, 1)
    b = occ_hop(own, -1, 0)
    a = occ_hop(own, 1, 0)
    columns = transposed(cabs_fit[0], slab_other)
    p0, a, b, columns, fock_other, keep_column, place = lax.optimization_barrier(
        (p0, a, b, columns, fock_other, keep_column, place)
    )

    def head(value):
        return lax.dynamic_slice_in_dim(value, (1 - side) * (half - HEAD), HEAD, 0)

    def tail(value):
        return lax.dynamic_slice_in_dim(value, side * HEAD, half - HEAD, 0)

    def onward(from_b, from_p0):
        return [
            occ_hop(from_b, 0, 1),
            occ_hop(from_p0, 1, 0),
            occ_hop(from_b, -1, 0),
            occ_hop(from_p0, 2, 0),
        ]

    heads = onward(head(b), head(p0))
    tails = onward(tail(b), tail(p0))

    def masked(keep, got, first):
        whole = (keep + got).astype(BF)
        mask = keep_column[first : first + keep.shape[0]]
        return jnp.where(mask[:, None], whole, jnp.zeros_like(whole))

    keep, send = fit_sums(place, [own, p0, a, b], columns)
    keep, *heads = lax.optimization_barrier((keep, *heads))
    got = aux_swap(send)
    got, *tails = lax.optimization_barrier((got, *tails))
    d_self, d_p0, d_a, d_b = masked(keep, got, 0)
    right_a = occ_hop(d_b, 1, 0)
    keep, send = fit_sums(place, heads, columns)
    got = aux_swap(send)
    (keep,) = fit_sums(place, tails, columns, keep)
    got, right_a = lax.optimization_barrier((got, right_a))
    d_pb, d_pa, d_c, d_pc = masked(keep, got, 4)
    takes_c = ((me & 1) ^ (me >> 2)) == 1
    d_px = jnp.where(takes_c, d_c, d_p0)
    d_given = jnp.where(takes_c, d_p0, d_c)

    left = jnp.concatenate([d_self, d_a, d_pa, d_px, d_pc], 0)
    cut = (left.shape[0] // 2 + 15) // 16 * 16
    rights = [(d_pb, lambda v: occ_hop(v, 1, 1)), (d_given, lambda v: px_hop(v, 1)), (d_pc, lambda v: occ_hop(v, 2, 1))]
    blocks = [(0, left)]
    up = down = left
    arrived = []
    for step in range(1, Z // 2):
        value, move = rights[step - 1]
        up, down, value = lax.optimization_barrier((up, down, value))
        up, down, value = lax.optimization_barrier((z_hop(up, 1), z_hop(down, -1), move(value)))
        arrived.append(value)
        blocks += [(-step, up), (step, down)]
    upper, lower = z_hop(up[:cut], 1), z_hop(down[cut:], -1)
    applied = apply_near(place, [o for o, _ in blocks], [v for _, v in blocks], fock, fock_other)
    row, to_a, to_pa, to_px = apply_last(
        place, applied, upper, lower, fock, fock_other, [d_self, right_a, *arrived]
    )
    row += occ_hop(to_a, -1, 0) + occ_hop(to_pa, -1, 1) + px_hop(to_px, 0)
    peers = 4 * Z
    spread = lax.all_to_all(
        jnp.broadcast_to(row, (peers, OCC)), ("cabs", "aux"), 0, 0, tiled=True
    )
    return jnp.sum(spread, axis=0)[None, :]


def solution(mesh):
    in_specs = (P("occ", None, "aux"), P("occ", "cabs", "aux"), P(None, "cabs"), P(), P())
    out_specs = P("occ", None)
    return jax.shard_map(shards, mesh=mesh, in_specs=in_specs, out_specs=out_specs, check_vma=False)
```

```python
import jax
import jax.numpy as jnp
from jax import lax
from jax.experimental import pallas as pl
from jax.experimental.pallas import tpu as pltpu
from jax.sharding import PartitionSpec as P

BF = jnp.bfloat16
F32 = jnp.float32
Y = 4
Z = 8
OCC = 2 * Y
KEPT = 40
STRIDE = 48
FOOT = 16
VMEM = pl.BlockSpec(memory_space=pltpu.VMEM)
SMEM = pl.BlockSpec(memory_space=pltpu.SMEM)
PARAMS = pltpu.CompilerParams(vmem_limit_bytes=8 * 2**20)

PLACES = ((0, 0), (0, 1), (-1, 0), (1, 0), (1, 1), (-1, 1), (2, 0), (2, 1))
LEFTS = ((0, 0), (0, 1), (-1, 0), (-1, 1), (2, 0), (2, 1))


def partner(me, dy, flip):
    return (((me >> 1) + dy) & (Y - 1)) * 2 + ((me & 1) ^ flip)


def occ_hop(value, dy, flip):
    return lax.ppermute(value, "occ", [(o, partner(o, dy, flip)) for o in range(OCC)])


def z_hop(value, dz):
    return lax.ppermute(value, "cabs", [(c, ((c // 2 + dz) % Z) * 2 + c % 2) for c in range(2 * Z)])


def core_swap(value):
    return lax.ppermute(value, "cabs", [(c, c ^ 1) for c in range(2 * Z)])


def aux_swap(value):
    return lax.ppermute(value, "aux", [(0, 1), (1, 0)])


def rows_dot(left, right):
    return lax.dot_general(left, right, (((1,), (1,)), ((), ())), preferred_element_type=F32)


def plain_dot(left, right):
    return lax.dot_general(left, right, (((1,), (0,)), ((), ())), preferred_element_type=F32)


def prepare(place, pair_block, block_rows, slab, slab_other):
    width, fit = slab.shape

    def body(place_ref, pair_ref, rows_ref, own_ref, other_ref, out_ref, mask_ref):
        out_ref[:, :width] = own_ref[...].T
        out_ref[:, width:] = other_ref[...].T
        me = place_ref[0]
        labels = rows_ref[pl.ds(place_ref[1], 1), :]
        first, second = labels[:, :width], labels[:, width:]
        swap = place_ref[2] == 1
        mine = jnp.where(swap, second, first)
        other = jnp.where(swap, first, second)
        for index, (dy, flip) in enumerate(PLACES):
            wanted = (pair_ref[me] + pair_ref[partner(me, dy, flip)]) & 1
            mask_ref[index : index + 1, :width] = jnp.where(mine == wanted, 1, 0)
            mask_ref[index : index + 1, width:] = jnp.where(other == wanted, 1, 0)

    return pl.pallas_call(
        body,
        out_shape=(
            jax.ShapeDtypeStruct((fit, 2 * width), BF),
            jax.ShapeDtypeStruct((len(PLACES), 2 * width), jnp.int32),
        ),
        in_specs=[SMEM, SMEM, VMEM, VMEM, VMEM],
        out_specs=(VMEM, VMEM),
        compiler_params=PARAMS,
        cost_estimate=pl.CostEstimate(
            flops=0, bytes_accessed=8 * fit * width, transcendentals=0
        ),
    )(place, pair_block, block_rows, slab, slab_other)


def fit_sums(place, parts, columns, scaled=False):
    count = len(parts)
    size = parts[0].shape[0]
    fit, width = columns.shape
    step = 2 * KEPT if size == 2 * KEPT else STRIDE
    shape = jax.ShapeDtypeStruct((count, KEPT, width), F32)
    if scaled:
        shapes = (jax.ShapeDtypeStruct((count * KEPT + FOOT, width), F32),)
    else:
        shapes = (shape, shape) if size == 2 * KEPT else (shape,)

    def body(place_ref, *refs):
        part_refs, columns_ref = refs[:count], refs[count]
        outs = refs[count + 1 : -2]
        stack_ref, total_ref = refs[-2:]
        for index in range(count):
            stack_ref[index * step : index * step + size, :] = part_refs[index][...]
        total_ref[...] = plain_dot(stack_ref[...], columns_ref[...])
        if size == 2 * KEPT:
            side = place_ref[3]
            for index in range(count):
                mine = pl.ds(pl.multiple_of(index * step + side * KEPT, 8), KEPT)
                other = pl.ds(pl.multiple_of(index * step + (1 - side) * KEPT, 8), KEPT)
                outs[0][index] = total_ref[mine, :]
                outs[1][index] = total_ref[other, :]
        elif not scaled:
            for index in range(count):
                outs[0][index] = total_ref[index * step : index * step + KEPT, :]
        else:
            blocks = [total_ref[index * step : index * step + KEPT, :] for index in range(count)]
            largest = jnp.max(jnp.abs(blocks[0]), axis=0, keepdims=True)
            for block in blocks[1:]:
                largest = jnp.maximum(largest, jnp.max(jnp.abs(block), axis=0, keepdims=True))
            largest = jnp.max(largest, axis=1, keepdims=True)
            exponent = jnp.floor(jnp.log2(jnp.maximum(largest, 1e-30)))
            scale = jnp.exp2(12.0 - exponent)
            for index in range(count):
                outs[0][index * KEPT : (index + 1) * KEPT, :] = blocks[index] * scale
            outs[0][count * KEPT :, :] = jnp.broadcast_to(exponent, (FOOT, width))

    return pl.pallas_call(
        body,
        out_shape=shapes,
        in_specs=[SMEM] + [VMEM] * (count + 1),
        out_specs=(VMEM,) * len(shapes),
        scratch_shapes=[pltpu.VMEM((count * step, fit), BF), pltpu.VMEM((count * step, width), F32)],
        compiler_params=PARAMS,
        cost_estimate=pl.CostEstimate(
            flops=2 * count * step * fit * width,
            bytes_accessed=2 * width * fit + 2 * count * size * fit + 8 * count * size * width,
            transcendentals=0,
        ),
    )(place, *parts, columns)


def apply_tile(place_ref, offset, block, own_ref, other_ref):
    width = own_ref.shape[1]
    own = other = None
    for index in range(2):
        row = (((place_ref[1] + offset) & (Z - 1)) * 2 + (place_ref[2] ^ index)) * width
        rows = pl.ds(pl.multiple_of(row, width), width)
        part = block[:, index * width : (index + 1) * width]
        to_own = plain_dot(part, own_ref[rows, :])
        to_other = plain_dot(part, other_ref[rows, :])
        own = to_own if own is None else own + to_own
        other = to_other if other is None else other + to_other
    return own, other


def apply_blocks(place, placed, fock, fock_other):
    offsets, blocks = zip(*placed)
    count = len(blocks)
    rows, columns = blocks[0].shape
    width = columns // 2

    def body(place_ref, *refs):
        own_ref, other_ref, out_ref = refs[count:]
        for index in range(count):
            own, other = apply_tile(
                place_ref, offsets[index], refs[index][...], own_ref, other_ref
            )
            if index == 0:
                out_ref[:, :width] = own
                out_ref[:, width:] = other
            else:
                out_ref[:, :width] += own
                out_ref[:, width:] += other

    return pl.pallas_call(
        body,
        out_shape=jax.ShapeDtypeStruct((rows, columns), F32),
        in_specs=[SMEM] + [VMEM] * (count + 2),
        out_specs=VMEM,
        compiler_params=PARAMS,
        cost_estimate=pl.CostEstimate(
            flops=2 * count * rows * columns * columns,
            bytes_accessed=2 * count * columns * (rows + columns),
            transcendentals=0,
        ),
    )(place, *blocks, fock, fock_other)


def apply_last(place, first_rows, applied, block, fock, fock_other, rights):
    rows, columns = applied.shape
    width = columns // 2

    def body(place_ref, first_ref, applied_ref, block_ref, own_ref, other_ref, *refs):
        right_refs, (row_ref, a_ref, pa_ref, sum_ref) = refs[:-4], refs[-4:]
        own, other = apply_tile(place_ref, Z // 2, block_ref[...], own_ref, other_ref)
        sum_ref[:, :width] = applied_ref[:, :width] + own
        sum_ref[:, width:] = applied_ref[:, width:] + other
        pieces = [ref[index] for ref in right_refs for index in range(ref.shape[0])]
        lefts = [
            ref[start : start + KEPT, :]
            for ref in (first_ref, sum_ref)
            for start in range(0, ref.shape[0], KEPT)
        ]
        sums = []
        for left, piece in zip(lefts, pieces):
            product = left * piece.astype(F32)
            sums.append(jnp.sum(jnp.sum(product, axis=0, keepdims=True), axis=1, keepdims=True))
        me = place_ref[0]
        lanes = lax.broadcasted_iota(jnp.int32, (1, OCC), 1)
        row = jnp.zeros((1, OCC), F32)
        for value, (dy, flip) in zip(sums, LEFTS):
            row += jnp.where(lanes == partner(me, dy, flip), value, 0.0)
        row_ref[...] = row
        here = lanes == me
        a_ref[...] = jnp.where(here, sums[2], 0.0)
        pa_ref[...] = jnp.where(here, sums[3], 0.0)

    shape = jax.ShapeDtypeStruct((1, OCC), F32)
    return pl.pallas_call(
        body,
        out_shape=(shape,) * 3,
        in_specs=[SMEM] + [VMEM] * (len(rights) + 5),
        out_specs=(VMEM,) * 3,
        scratch_shapes=[pltpu.VMEM((rows, columns), F32)],
        compiler_params=PARAMS,
        cost_estimate=pl.CostEstimate(
            flops=2 * rows * columns * columns,
            bytes_accessed=2 * columns * (rows + columns) + 6 * rows * columns,
            transcendentals=0,
        ),
    )(place, first_rows, applied, block, fock, fock_other, *rights)


def shards(occ_fit, cabs_fit, fock, cabs_block, pair_block):
    me = lax.axis_index("occ")
    cabs = lax.axis_index("cabs")
    side = lax.axis_index("aux")
    core = cabs & 1
    z = cabs >> 1
    place = jnp.stack([me, z, core, side]).astype(jnp.int32)
    m_rows = occ_fit.shape[1]
    width = cabs_fit.shape[1]
    half = m_rows // 2

    own = lax.dynamic_slice_in_dim(occ_fit[0], core * half, half, 0)
    slab_other = core_swap(cabs_fit[0])
    fock_other = core_swap(fock)

    p0, a, b = occ_hop(own, 0, 1), occ_hop(own, 1, 0), occ_hop(own, -1, 0)
    columns, keep_column = prepare(
        place, pair_block, cabs_block.reshape(Z, 2 * width), cabs_fit[0], slab_other
    )
    p0, a, b, columns, fock_other = lax.optimization_barrier((p0, a, b, columns, fock_other))

    def head(value):
        return lax.dynamic_slice_in_dim(value, (1 - side) * KEPT, KEPT, 0)

    def tail(value):
        return lax.dynamic_slice_in_dim(value, side * KEPT, KEPT, 0)

    def second_round(p0, b):
        return occ_hop(b, 0, 1), occ_hop(p0, 1, 0), occ_hop(b, -1, 0), occ_hop(p0, 2, 0)

    heads = second_round(head(p0), head(b))
    tails = second_round(tail(p0), tail(b))

    def masked(keep, got, first):
        whole = (keep + got).astype(BF)
        mask = keep_column[first : first + keep.shape[0]]
        return jnp.where(mask[:, None] != 0, whole, jnp.zeros_like(whole))

    keep, send = fit_sums(place, [own, p0, a, b], columns)
    keep, *heads = lax.optimization_barrier((keep, *heads))
    got = aux_swap(send)
    got, *tails = lax.optimization_barrier((got, *tails))
    near = masked(keep, got, 0)
    (send,) = fit_sums(place, heads, columns, True)
    got = aux_swap(send.astype(jnp.float16))
    (keep,) = fit_sums(place, tails, columns)
    unscale = jnp.exp2(got[-1:].astype(F32) - 12.0)
    got = (got[:-FOOT].astype(F32) * unscale).reshape(keep.shape)
    far = masked(keep, got, 4)

    first = jnp.concatenate([near[0], near[1], near[2]], 0)
    second = jnp.concatenate([far[1], far[2], far[3]], 0)
    first_blocks, second_blocks = [(0, first)], [(0, second)]

    def ring_step(step, up, down, blocks):
        up, down = z_hop(up, 1), z_hop(down, -1)
        blocks.extend([(-step, up), (step, down)])
        return up, down

    rights = [jnp.stack([near[1], far[0], far[3]])]
    moves = [(0, 1), (1, 0), (2, 0)]
    up_a = down_a = first
    up_b = down_b = second
    for step in range(1, Z // 2):
        up_a, down_a = ring_step(step, up_a, down_a, first_blocks)
        up_b, down_b, value = lax.optimization_barrier((up_b, down_b, rights[-1]))
        up_b, down_b = ring_step(step, up_b, down_b, second_blocks)
        value = occ_hop(value, *moves[step - 1])
        up_b, down_b, value = lax.optimization_barrier((up_b, down_b, value))
        rights[-1] = value
        if step == 1:
            rights.append(jnp.stack([near[3], value[1]]))
        elif step == 2:
            rights.append(jnp.stack([far[2], rights[0][2]]))
    first_blocks.append((Z // 2, z_hop(up_a, 1)))
    block = z_hop(down_b, -1)
    first = apply_blocks(place, first_blocks, fock, fock_other)
    second = apply_blocks(place, second_blocks, fock, fock_other)
    rights = [near[:1], rights[0][:1], *rights[1:]]
    row, to_a, to_pa = apply_last(place, first, second, block, fock, fock_other, rights)
    row += occ_hop(to_a, -1, 0) + occ_hop(to_pa, -1, 1)
    peers = 4 * Z
    spread = lax.all_to_all(
        jnp.broadcast_to(row, (peers, OCC)), ("cabs", "aux"), 0, 0, tiled=True
    )
    return jnp.sum(spread, axis=0)[None, :]


def solution(mesh):
    in_specs = (P("occ", None, "aux"), P("occ", "cabs", "aux"), P(None, "cabs"), P(), P())
    out_specs = P("occ", None)
    return jax.shard_map(shards, mesh=mesh, in_specs=in_specs, out_specs=out_specs, check_vma=False)
```

```python
import jax
import jax.numpy as jnp
from jax import lax
from jax.experimental import pallas as pl
from jax.experimental.pallas import tpu as pltpu
from jax.sharding import PartitionSpec as P

BF = jnp.bfloat16
F32 = jnp.float32
Y = 4
Z = 8
OCC = 2 * Y
KEPT = 40
STRIDE = 48
FOOT = 16
VMEM = pl.BlockSpec(memory_space=pltpu.VMEM)
SMEM = pl.BlockSpec(memory_space=pltpu.SMEM)
PARAMS = pltpu.CompilerParams(vmem_limit_bytes=8 * 2**20)

PLACES = ((0, 0), (0, 1), (-1, 0), (1, 0), (1, 1), (-1, 1), (2, 0), (2, 1))
FIRST = ((0, 1), (-1, 0), (-1, 1))
SECOND = ((0, 0), (2, 0), (2, 1))


def partner(me, dy, flip):
    return (((me >> 1) + dy) & (Y - 1)) * 2 + ((me & 1) ^ flip)


def occ_hop(value, dy, flip):
    return lax.ppermute(value, "occ", [(o, partner(o, dy, flip)) for o in range(OCC)])


def z_hop(value, dz):
    return lax.ppermute(value, "cabs", [(c, ((c // 2 + dz) % Z) * 2 + c % 2) for c in range(2 * Z)])


def core_swap(value):
    return lax.ppermute(value, "cabs", [(c, c ^ 1) for c in range(2 * Z)])


def aux_swap(value):
    return lax.ppermute(value, "aux", [(0, 1), (1, 0)])


def rows_dot(left, right):
    return lax.dot_general(left, right, (((1,), (1,)), ((), ())), preferred_element_type=F32)


def plain_dot(left, right):
    return lax.dot_general(left, right, (((1,), (0,)), ((), ())), preferred_element_type=F32)


def prepare(place, pair_block, block_rows, slab, slab_other):
    width, fit = slab.shape

    def body(place_ref, pair_ref, rows_ref, own_ref, other_ref, out_ref, mask_ref):
        out_ref[:, :width] = own_ref[...].T
        out_ref[:, width:] = other_ref[...].T
        me = place_ref[0]
        labels = rows_ref[pl.ds(place_ref[1], 1), :]
        first, second = labels[:, :width], labels[:, width:]
        swap = place_ref[2] == 1
        mine = jnp.where(swap, second, first)
        other = jnp.where(swap, first, second)
        for index, (dy, flip) in enumerate(PLACES):
            wanted = (pair_ref[me] + pair_ref[partner(me, dy, flip)]) & 1
            mask_ref[index : index + 1, :width] = jnp.where(mine == wanted, 1, 0)
            mask_ref[index : index + 1, width:] = jnp.where(other == wanted, 1, 0)

    return pl.pallas_call(
        body,
        out_shape=(
            jax.ShapeDtypeStruct((fit, 2 * width), BF),
            jax.ShapeDtypeStruct((len(PLACES), 2 * width), jnp.int32),
        ),
        in_specs=[SMEM, SMEM, VMEM, VMEM, VMEM],
        out_specs=(VMEM, VMEM),
        compiler_params=PARAMS,
        cost_estimate=pl.CostEstimate(
            flops=0, bytes_accessed=8 * fit * width, transcendentals=0
        ),
    )(place, pair_block, block_rows, slab, slab_other)


def fit_sums(place, parts, columns, scaled=False):
    count = len(parts)
    size = parts[0].shape[0]
    fit, width = columns.shape
    step = 2 * KEPT if size == 2 * KEPT else STRIDE
    shape = jax.ShapeDtypeStruct((count, KEPT, width), F32)
    if scaled:
        shapes = (jax.ShapeDtypeStruct((count * KEPT + FOOT, width), F32),)
    else:
        shapes = (shape, shape) if size == 2 * KEPT else (shape,)

    def body(place_ref, *refs):
        part_refs, columns_ref = refs[:count], refs[count]
        outs = refs[count + 1 : -2]
        stack_ref, total_ref = refs[-2:]
        for index in range(count):
            stack_ref[index * step : index * step + size, :] = part_refs[index][...]
        total_ref[...] = plain_dot(stack_ref[...], columns_ref[...])
        if size == 2 * KEPT:
            side = place_ref[3]
            for index in range(count):
                mine = pl.ds(pl.multiple_of(index * step + side * KEPT, 8), KEPT)
                other = pl.ds(pl.multiple_of(index * step + (1 - side) * KEPT, 8), KEPT)
                outs[0][index] = total_ref[mine, :]
                outs[1][index] = total_ref[other, :]
        elif not scaled:
            for index in range(count):
                outs[0][index] = total_ref[index * step : index * step + KEPT, :]
        else:
            blocks = [total_ref[index * step : index * step + KEPT, :] for index in range(count)]
            largest = jnp.max(jnp.abs(blocks[0]), axis=0, keepdims=True)
            for block in blocks[1:]:
                largest = jnp.maximum(largest, jnp.max(jnp.abs(block), axis=0, keepdims=True))
            largest = jnp.max(largest, axis=1, keepdims=True)
            exponent = jnp.floor(jnp.log2(jnp.maximum(largest, 1e-30)))
            scale = jnp.exp2(12.0 - exponent)
            for index in range(count):
                outs[0][index * KEPT : (index + 1) * KEPT, :] = blocks[index] * scale
            outs[0][count * KEPT :, :] = jnp.broadcast_to(exponent, (FOOT, width))

    return pl.pallas_call(
        body,
        out_shape=shapes,
        in_specs=[SMEM] + [VMEM] * (count + 1),
        out_specs=(VMEM,) * len(shapes),
        scratch_shapes=[pltpu.VMEM((count * step, fit), BF), pltpu.VMEM((count * step, width), F32)],
        compiler_params=PARAMS,
        cost_estimate=pl.CostEstimate(
            flops=2 * count * step * fit * width,
            bytes_accessed=2 * width * fit + 2 * count * size * fit + 8 * count * size * width,
            transcendentals=0,
        ),
    )(place, *parts, columns)


def apply_tile(place_ref, offset, block, own_ref, other_ref):
    width = own_ref.shape[1]
    own = other = None
    for index in range(2):
        row = (((place_ref[1] + offset) & (Z - 1)) * 2 + (place_ref[2] ^ index)) * width
        rows = pl.ds(pl.multiple_of(row, width), width)
        part = block[:, index * width : (index + 1) * width]
        to_own = plain_dot(part, own_ref[rows, :])
        to_other = plain_dot(part, other_ref[rows, :])
        own = to_own if own is None else own + to_own
        other = to_other if other is None else other + to_other
    return own, other


def apply_blocks(place, placed, fock, fock_other):
    offsets, blocks = zip(*placed)
    count = len(blocks)
    rows, columns = blocks[0].shape
    width = columns // 2

    def body(place_ref, *refs):
        own_ref, other_ref, out_ref = refs[count:]
        for index in range(count):
            own, other = apply_tile(
                place_ref, offsets[index], refs[index][...], own_ref, other_ref
            )
            if index == 0:
                out_ref[:, :width] = own
                out_ref[:, width:] = other
            else:
                out_ref[:, :width] += own
                out_ref[:, width:] += other

    return pl.pallas_call(
        body,
        out_shape=jax.ShapeDtypeStruct((rows, columns), F32),
        in_specs=[SMEM] + [VMEM] * (count + 2),
        out_specs=VMEM,
        compiler_params=PARAMS,
        cost_estimate=pl.CostEstimate(
            flops=2 * count * rows * columns * columns,
            bytes_accessed=2 * count * columns * (rows + columns),
            transcendentals=0,
        ),
    )(place, *blocks, fock, fock_other)


def contract(place, applied, placed, fock, fock_other, rights, pairs, mirrored):
    offsets, blocks = zip(*placed)
    rows, columns = blocks[0].shape
    width = columns // 2
    count = len(blocks)
    known = [] if applied is None else [applied]

    def body(place_ref, *refs):
        block_refs, (own_ref, other_ref) = refs[:count], refs[count : count + 2]
        known_refs = refs[count + 2 : count + 2 + len(known)]
        right_refs = refs[count + 2 + len(known) : count + 2 + len(known) + len(rights)]
        outs, sum_ref = refs[count + 2 + len(known) + len(rights) : -1], refs[-1]
        for index in range(count):
            own, other = apply_tile(
                place_ref, offsets[index], block_refs[index][...], own_ref, other_ref
            )
            if index == 0 and known:
                own += known_refs[0][:, :width]
                other += known_refs[0][:, width:]
            elif index > 0:
                own += sum_ref[:, :width]
                other += sum_ref[:, width:]
            sum_ref[:, :width] = own
            sum_ref[:, width:] = other
        pieces = [ref[index] for ref in right_refs for index in range(ref.shape[0])]
        sums = []
        for index, piece in enumerate(pieces):
            product = sum_ref[index * KEPT : (index + 1) * KEPT, :] * piece.astype(F32)
            sums.append(jnp.sum(jnp.sum(product, axis=0, keepdims=True), axis=1, keepdims=True))
        me = place_ref[0]
        lanes = lax.broadcasted_iota(jnp.int32, (1, OCC), 1)
        row = jnp.zeros((1, OCC), F32)
        for value, (dy, flip) in zip(sums, pairs):
            row += jnp.where(lanes == partner(me, dy, flip), value, 0.0)
        outs[0][...] = row
        for out, index in zip(outs[1:], mirrored):
            out[...] = jnp.where(lanes == me, sums[index], 0.0)

    shapes = (jax.ShapeDtypeStruct((1, OCC), F32),) * (1 + len(mirrored))
    return pl.pallas_call(
        body,
        out_shape=shapes,
        in_specs=[SMEM] + [VMEM] * (count + 2 + len(known) + len(rights)),
        out_specs=(VMEM,) * len(shapes),
        scratch_shapes=[pltpu.VMEM((rows, columns), F32)],
        compiler_params=PARAMS,
        cost_estimate=pl.CostEstimate(
            flops=2 * count * rows * columns * columns,
            bytes_accessed=2 * count * columns * (rows + columns) + 6 * rows * columns,
            transcendentals=0,
        ),
    )(place, *blocks, fock, fock_other, *known, *rights)


def shards(occ_fit, cabs_fit, fock, cabs_block, pair_block):
    me = lax.axis_index("occ")
    cabs = lax.axis_index("cabs")
    side = lax.axis_index("aux")
    core = cabs & 1
    z = cabs >> 1
    place = jnp.stack([me, z, core, side]).astype(jnp.int32)
    m_rows = occ_fit.shape[1]
    width = cabs_fit.shape[1]
    half = m_rows // 2

    own = lax.dynamic_slice_in_dim(occ_fit[0], core * half, half, 0)
    slab_other = core_swap(cabs_fit[0])
    fock_other = core_swap(fock)

    p0, a, b = occ_hop(own, 0, 1), occ_hop(own, 1, 0), occ_hop(own, -1, 0)
    columns, keep_column = prepare(
        place, pair_block, cabs_block.reshape(Z, 2 * width), cabs_fit[0], slab_other
    )
    p0, a, b, columns, fock_other = lax.optimization_barrier((p0, a, b, columns, fock_other))

    def head(value):
        return lax.dynamic_slice_in_dim(value, (1 - side) * KEPT, KEPT, 0)

    def tail(value):
        return lax.dynamic_slice_in_dim(value, side * KEPT, KEPT, 0)

    def second_round(p0, b):
        return occ_hop(b, 0, 1), occ_hop(p0, 1, 0), occ_hop(b, -1, 0), occ_hop(p0, 2, 0)

    heads = second_round(head(p0), head(b))
    tails = second_round(tail(p0), tail(b))

    def masked(keep, got, first):
        whole = (keep + got).astype(BF)
        mask = keep_column[first : first + keep.shape[0]]
        return jnp.where(mask[:, None] != 0, whole, jnp.zeros_like(whole))

    keep, send = fit_sums(place, [own, p0, a, b], columns)
    keep, *heads = lax.optimization_barrier((keep, *heads))
    got = aux_swap(send)
    got, *tails = lax.optimization_barrier((got, *tails))
    near = masked(keep, got, 0)
    (send,) = fit_sums(place, heads, columns, True)
    got = aux_swap(send.astype(jnp.float16))
    (keep,) = fit_sums(place, tails, columns)
    unscale = jnp.exp2(got[-1:].astype(F32) - 12.0)
    got = (got[:-FOOT].astype(F32) * unscale).reshape(keep.shape)
    far = masked(keep, got, 4)

    first = jnp.concatenate([near[1], near[2], far[1]], 0)
    second = jnp.concatenate([near[0], far[2], far[3]], 0)
    first_blocks, second_blocks = [(0, first)], [(0, second)]

    def ring_step(step, up, down, blocks):
        up, down = z_hop(up, 1), z_hop(down, -1)
        blocks.extend([(-step, up), (step, down)])
        return up, down

    rights = [jnp.stack([near[1], far[0], far[3]])]
    moves = [(0, 1), (1, 0), (2, 0)]
    up_a = down_a = first
    up_b = down_b = second
    for step in range(1, Z // 2):
        up_a, down_a, value = lax.optimization_barrier((up_a, down_a, rights[-1]))
        up_a, down_a = ring_step(step, up_a, down_a, first_blocks)
        value = occ_hop(value, *moves[step - 1])
        up_a, down_a, value = lax.optimization_barrier((up_a, down_a, value))
        up_b, down_b = ring_step(step, up_b, down_b, second_blocks)
        rights[-1] = value
        if step == 1:
            rights.append(jnp.stack([near[3], value[1]]))
        elif step == 2:
            rights.append(jnp.stack([far[2], rights[0][2]]))
    first_blocks.append((Z // 2, z_hop(up_a, 1)))
    last_block = [(Z // 2, z_hop(down_b, -1))]
    row, to_a, to_pa = contract(
        place, None, first_blocks, fock, fock_other, [rights[0][:1], rights[1]], FIRST, (1, 2)
    )
    second = apply_blocks(place, second_blocks, fock, fock_other)
    (rest,) = contract(
        place, second, last_block, fock, fock_other, [near[:1], rights[2]], SECOND, ()
    )
    row += rest + occ_hop(to_a, -1, 0) + occ_hop(to_pa, -1, 1)
    peers = 4 * Z
    spread = lax.all_to_all(
        jnp.broadcast_to(row, (peers, OCC)), ("cabs", "aux"), 0, 0, tiled=True
    )
    return jnp.sum(spread, axis=0)[None, :]


def solution(mesh):
    in_specs = (P("occ", None, "aux"), P("occ", "cabs", "aux"), P(None, "cabs"), P(), P())
    out_specs = P("occ", None)
    return jax.shard_map(shards, mesh=mesh, in_specs=in_specs, out_specs=out_specs, check_vma=False)
```

```python
import jax
import jax.numpy as jnp
from jax import lax
from jax.experimental import pallas as pl
from jax.experimental.pallas import tpu as pltpu
from jax.sharding import PartitionSpec as P

BF = jnp.bfloat16
F32 = jnp.float32
Y = 4
Z = 8
OCC = 2 * Y
KEPT = 40
STRIDE = 48
FOOT = 16
VMEM = pl.BlockSpec(memory_space=pltpu.VMEM)
SMEM = pl.BlockSpec(memory_space=pltpu.SMEM)
PARAMS = pltpu.CompilerParams(vmem_limit_bytes=8 * 2**20)

PLACES = ((0, 0), (0, 1), (-1, 0), (1, 0), (1, 1), (-1, 1), (2, 0), (2, 1))
FIRST = ((0, 1), (-1, 0), (-1, 1))
SECOND = ((0, 0), (2, 0), (2, 1))


def partner(me, dy, flip):
    return (((me >> 1) + dy) & (Y - 1)) * 2 + ((me & 1) ^ flip)


def occ_hop(value, dy, flip):
    return lax.ppermute(value, "occ", [(o, partner(o, dy, flip)) for o in range(OCC)])


def z_hop(value, dz):
    return lax.ppermute(value, "cabs", [(c, ((c // 2 + dz) % Z) * 2 + c % 2) for c in range(2 * Z)])


def core_swap(value):
    return lax.ppermute(value, "cabs", [(c, c ^ 1) for c in range(2 * Z)])


def aux_swap(value):
    return lax.ppermute(value, "aux", [(0, 1), (1, 0)])


def rows_dot(left, right):
    return lax.dot_general(left, right, (((1,), (1,)), ((), ())), preferred_element_type=F32)


def plain_dot(left, right):
    return lax.dot_general(left, right, (((1,), (0,)), ((), ())), preferred_element_type=F32)


def own_rows(place, occ_fit, size):
    fit = occ_fit.shape[2]

    def body(place_ref, rows_ref, out_ref, sem):
        first = pl.multiple_of(place_ref[2] * size, 16)
        copy = pltpu.make_async_copy(rows_ref.at[0, pl.ds(first, size), :], out_ref, sem)
        copy.start()
        copy.wait()

    return pl.pallas_call(
        body,
        out_shape=jax.ShapeDtypeStruct((size, fit), BF),
        in_specs=[SMEM, pl.BlockSpec(memory_space=pl.ANY)],
        out_specs=VMEM,
        scratch_shapes=[pltpu.SemaphoreType.DMA],
        compiler_params=PARAMS,
        cost_estimate=pl.CostEstimate(flops=0, bytes_accessed=4 * size * fit, transcendentals=0),
    )(place, occ_fit)


def prepare(place, pair_block, block_rows, slab, slab_other):
    width, fit = slab.shape

    def body(place_ref, pair_ref, rows_ref, own_ref, other_ref, out_ref, mask_ref):
        out_ref[:, :width] = own_ref[...].T
        out_ref[:, width:] = other_ref[...].T
        me = place_ref[0]
        labels = rows_ref[pl.ds(place_ref[1], 1), :]
        first, second = labels[:, :width], labels[:, width:]
        swap = place_ref[2] == 1
        mine = jnp.where(swap, second, first)
        other = jnp.where(swap, first, second)
        for index, (dy, flip) in enumerate(PLACES):
            wanted = (pair_ref[me] + pair_ref[partner(me, dy, flip)]) & 1
            mask_ref[index : index + 1, :width] = jnp.where(mine == wanted, 1, 0)
            mask_ref[index : index + 1, width:] = jnp.where(other == wanted, 1, 0)

    return pl.pallas_call(
        body,
        out_shape=(
            jax.ShapeDtypeStruct((fit, 2 * width), BF),
            jax.ShapeDtypeStruct((len(PLACES), 2 * width), jnp.int32),
        ),
        in_specs=[SMEM, SMEM, VMEM, VMEM, VMEM],
        out_specs=(VMEM, VMEM),
        compiler_params=PARAMS,
        cost_estimate=pl.CostEstimate(
            flops=0, bytes_accessed=8 * fit * width, transcendentals=0
        ),
    )(place, pair_block, block_rows, slab, slab_other)


def fit_sums(place, parts, columns, scaled=False):
    count = len(parts)
    size = parts[0].shape[0]
    fit, width = columns.shape
    step = 2 * KEPT if size == 2 * KEPT else STRIDE
    shape = jax.ShapeDtypeStruct((count, KEPT, width), F32)
    if scaled:
        shapes = (jax.ShapeDtypeStruct((count * KEPT + FOOT, width), F32),)
    else:
        shapes = (shape, shape) if size == 2 * KEPT else (shape,)

    def body(place_ref, *refs):
        part_refs, columns_ref = refs[:count], refs[count]
        outs = refs[count + 1 : -2]
        stack_ref, total_ref = refs[-2:]
        for index in range(count):
            stack_ref[index * step : index * step + size, :] = part_refs[index][...]
        total_ref[...] = plain_dot(stack_ref[...], columns_ref[...])
        if size == 2 * KEPT:
            side = place_ref[3]
            for index in range(count):
                mine = pl.ds(pl.multiple_of(index * step + side * KEPT, 8), KEPT)
                other = pl.ds(pl.multiple_of(index * step + (1 - side) * KEPT, 8), KEPT)
                outs[0][index] = total_ref[mine, :]
                outs[1][index] = total_ref[other, :]
        elif not scaled:
            for index in range(count):
                outs[0][index] = total_ref[index * step : index * step + KEPT, :]
        else:
            blocks = [total_ref[index * step : index * step + KEPT, :] for index in range(count)]
            largest = jnp.max(jnp.abs(blocks[0]), axis=0, keepdims=True)
            for block in blocks[1:]:
                largest = jnp.maximum(largest, jnp.max(jnp.abs(block), axis=0, keepdims=True))
            largest = jnp.max(largest, axis=1, keepdims=True)
            exponent = jnp.floor(jnp.log2(jnp.maximum(largest, 1e-30)))
            scale = jnp.exp2(12.0 - exponent)
            for index in range(count):
                outs[0][index * KEPT : (index + 1) * KEPT, :] = blocks[index] * scale
            outs[0][count * KEPT :, :] = jnp.broadcast_to(exponent, (FOOT, width))

    return pl.pallas_call(
        body,
        out_shape=shapes,
        in_specs=[SMEM] + [VMEM] * (count + 1),
        out_specs=(VMEM,) * len(shapes),
        scratch_shapes=[pltpu.VMEM((count * step, fit), BF), pltpu.VMEM((count * step, width), F32)],
        compiler_params=PARAMS,
        cost_estimate=pl.CostEstimate(
            flops=2 * count * step * fit * width,
            bytes_accessed=2 * width * fit + 2 * count * size * fit + 8 * count * size * width,
            transcendentals=0,
        ),
    )(place, *parts, columns)


def apply_tile(place_ref, offset, block, own_ref, other_ref):
    width = own_ref.shape[1]
    own = other = None
    for index in range(2):
        row = (((place_ref[1] + offset) & (Z - 1)) * 2 + (place_ref[2] ^ index)) * width
        rows = pl.ds(pl.multiple_of(row, width), width)
        part = block[:, index * width : (index + 1) * width]
        to_own = plain_dot(part, own_ref[rows, :])
        to_other = plain_dot(part, other_ref[rows, :])
        own = to_own if own is None else own + to_own
        other = to_other if other is None else other + to_other
    return own, other


def apply_blocks(place, placed, fock, fock_other):
    offsets, blocks = zip(*placed)
    count = len(blocks)
    rows, columns = blocks[0].shape
    width = columns // 2

    def body(place_ref, *refs):
        own_ref, other_ref, out_ref = refs[count:]
        for index in range(count):
            own, other = apply_tile(
                place_ref, offsets[index], refs[index][...], own_ref, other_ref
            )
            if index == 0:
                out_ref[:, :width] = own
                out_ref[:, width:] = other
            else:
                out_ref[:, :width] += own
                out_ref[:, width:] += other

    return pl.pallas_call(
        body,
        out_shape=jax.ShapeDtypeStruct((rows, columns), F32),
        in_specs=[SMEM] + [VMEM] * (count + 2),
        out_specs=VMEM,
        compiler_params=PARAMS,
        cost_estimate=pl.CostEstimate(
            flops=2 * count * rows * columns * columns,
            bytes_accessed=2 * count * columns * (rows + columns),
            transcendentals=0,
        ),
    )(place, *blocks, fock, fock_other)


def contract(place, applied, placed, fock, fock_other, rights, pairs, mirrored):
    offsets, blocks = zip(*placed)
    rows, columns = blocks[0].shape
    width = columns // 2
    count = len(blocks)
    known = [] if applied is None else [applied]

    def body(place_ref, *refs):
        block_refs, (own_ref, other_ref) = refs[:count], refs[count : count + 2]
        known_refs = refs[count + 2 : count + 2 + len(known)]
        right_refs = refs[count + 2 + len(known) : count + 2 + len(known) + len(rights)]
        outs, sum_ref = refs[count + 2 + len(known) + len(rights) : -1], refs[-1]
        for index in range(count):
            own, other = apply_tile(
                place_ref, offsets[index], block_refs[index][...], own_ref, other_ref
            )
            if index == 0 and known:
                own += known_refs[0][:, :width]
                other += known_refs[0][:, width:]
            elif index > 0:
                own += sum_ref[:, :width]
                other += sum_ref[:, width:]
            sum_ref[:, :width] = own
            sum_ref[:, width:] = other
        pieces = [ref[index] for ref in right_refs for index in range(ref.shape[0])]
        sums = []
        for index, piece in enumerate(pieces):
            product = sum_ref[index * KEPT : (index + 1) * KEPT, :] * piece.astype(F32)
            sums.append(jnp.sum(jnp.sum(product, axis=0, keepdims=True), axis=1, keepdims=True))
        me = place_ref[0]
        lanes = lax.broadcasted_iota(jnp.int32, (1, OCC), 1)
        row = jnp.zeros((1, OCC), F32)
        for value, (dy, flip) in zip(sums, pairs):
            row += jnp.where(lanes == partner(me, dy, flip), value, 0.0)
        outs[0][...] = row
        for out, index in zip(outs[1:], mirrored):
            out[...] = jnp.where(lanes == me, sums[index], 0.0)

    shapes = (jax.ShapeDtypeStruct((1, OCC), F32),) * (1 + len(mirrored))
    return pl.pallas_call(
        body,
        out_shape=shapes,
        in_specs=[SMEM] + [VMEM] * (count + 2 + len(known) + len(rights)),
        out_specs=(VMEM,) * len(shapes),
        scratch_shapes=[pltpu.VMEM((rows, columns), F32)],
        compiler_params=PARAMS,
        cost_estimate=pl.CostEstimate(
            flops=2 * count * rows * columns * columns,
            bytes_accessed=2 * count * columns * (rows + columns) + 6 * rows * columns,
            transcendentals=0,
        ),
    )(place, *blocks, fock, fock_other, *known, *rights)


def shards(occ_fit, cabs_fit, fock, cabs_block, pair_block):
    me = lax.axis_index("occ")
    cabs = lax.axis_index("cabs")
    side = lax.axis_index("aux")
    core = cabs & 1
    z = cabs >> 1
    place = jnp.stack([me, z, core, side]).astype(jnp.int32)
    m_rows = occ_fit.shape[1]
    width = cabs_fit.shape[1]
    half = m_rows // 2

    own = own_rows(place, occ_fit, half)
    slab_other = core_swap(cabs_fit[0])
    fock_other = core_swap(fock)

    p0, a, b = occ_hop(own, 0, 1), occ_hop(own, 1, 0), occ_hop(own, -1, 0)
    columns, keep_column = prepare(
        place, pair_block, cabs_block.reshape(Z, 2 * width), cabs_fit[0], slab_other
    )
    p0, a, b, columns, fock_other = lax.optimization_barrier((p0, a, b, columns, fock_other))

    def head(value):
        return lax.dynamic_slice_in_dim(value, (1 - side) * KEPT, KEPT, 0)

    def tail(value):
        return lax.dynamic_slice_in_dim(value, side * KEPT, KEPT, 0)

    def second_round(p0, b):
        return occ_hop(b, 0, 1), occ_hop(p0, 1, 0), occ_hop(b, -1, 0), occ_hop(p0, 2, 0)

    heads = second_round(head(p0), head(b))
    tails = second_round(tail(p0), tail(b))

    def masked(keep, got, first):
        whole = (keep + got).astype(BF)
        mask = keep_column[first : first + keep.shape[0]]
        return jnp.where(mask[:, None] != 0, whole, jnp.zeros_like(whole))

    keep, send = fit_sums(place, [own, p0, a, b], columns)
    keep, *heads = lax.optimization_barrier((keep, *heads))
    got = aux_swap(send)
    got, *tails = lax.optimization_barrier((got, *tails))
    near = masked(keep, got, 0)
    (send,) = fit_sums(place, heads, columns, True)
    got = aux_swap(send.astype(jnp.float16))
    (keep,) = fit_sums(place, tails, columns)
    unscale = jnp.exp2(got[-1:].astype(F32) - 12.0)
    got = (got[:-FOOT].astype(F32) * unscale).reshape(keep.shape)
    far = masked(keep, got, 4)

    first = jnp.concatenate([near[1], near[2], far[1]], 0)
    second = jnp.concatenate([near[0], far[2], far[3]], 0)
    first_blocks, second_blocks = [(0, first)], [(0, second)]

    def ring_step(step, up, down, blocks):
        up, down = z_hop(up, 1), z_hop(down, -1)
        blocks.extend([(-step, up), (step, down)])
        return up, down

    rights = [jnp.stack([near[1], far[0], far[3]])]
    moves = [(0, 1), (1, 0), (2, 0)]
    up_a = down_a = first
    up_b = down_b = second
    for step in range(1, Z // 2):
        up_a, down_a, value = lax.optimization_barrier((up_a, down_a, rights[-1]))
        up_a, down_a = ring_step(step, up_a, down_a, first_blocks)
        value = occ_hop(value, *moves[step - 1])
        up_a, down_a, value = lax.optimization_barrier((up_a, down_a, value))
        up_b, down_b = ring_step(step, up_b, down_b, second_blocks)
        rights[-1] = value
        if step == 1:
            rights.append(jnp.stack([near[3], value[1]]))
        elif step == 2:
            rights.append(jnp.stack([far[2], rights[0][2]]))
    first_blocks.append((Z // 2, z_hop(up_a, 1)))
    last_block = [(Z // 2, z_hop(down_b, -1))]
    row, to_a, to_pa = contract(
        place, None, first_blocks, fock, fock_other, [rights[0][:1], rights[1]], FIRST, (1, 2)
    )
    second = apply_blocks(place, second_blocks, fock, fock_other)
    (rest,) = contract(
        place, second, last_block, fock, fock_other, [near[:1], rights[2]], SECOND, ()
    )
    row += rest + occ_hop(to_a, -1, 0) + occ_hop(to_pa, -1, 1)
    peers = 4 * Z
    spread = lax.all_to_all(
        jnp.broadcast_to(row, (peers, OCC)), ("cabs", "aux"), 0, 0, tiled=True
    )
    return jnp.sum(spread, axis=0)[None, :]


def solution(mesh):
    in_specs = (P("occ", None, "aux"), P("occ", "cabs", "aux"), P(None, "cabs"), P(), P())
    out_specs = P("occ", None)
    return jax.shard_map(shards, mesh=mesh, in_specs=in_specs, out_specs=out_specs, check_vma=False)
```

```python
import jax
import jax.numpy as jnp
from jax import lax
from jax.experimental import pallas as pl
from jax.experimental.pallas import tpu as pltpu
from jax.sharding import PartitionSpec as P

BF = jnp.bfloat16
F32 = jnp.float32
Y = 4
Z = 8
OCC = 2 * Y
KEPT = 40
STRIDE = 48
FOOT = 16
VMEM = pl.BlockSpec(memory_space=pltpu.VMEM)
SMEM = pl.BlockSpec(memory_space=pltpu.SMEM)
PARAMS = pltpu.CompilerParams(vmem_limit_bytes=8 * 2**20)

PLACES = ((0, 0), (0, 1), (-1, 0), (1, 0), (1, 1), (-1, 1), (2, 0), (2, 1))
FIRST = ((0, 1), (-1, 0), (-1, 1))
SECOND = ((0, 0), (2, 0), (2, 1))


def partner(me, dy, flip):
    return (((me >> 1) + dy) & (Y - 1)) * 2 + ((me & 1) ^ flip)


def occ_hop(value, dy, flip):
    return lax.ppermute(value, "occ", [(o, partner(o, dy, flip)) for o in range(OCC)])


def z_hop(value, dz):
    return lax.ppermute(value, "cabs", [(c, ((c // 2 + dz) % Z) * 2 + c % 2) for c in range(2 * Z)])


def core_swap(value):
    return lax.ppermute(value, "cabs", [(c, c ^ 1) for c in range(2 * Z)])


def aux_swap(value):
    return lax.ppermute(value, "aux", [(0, 1), (1, 0)])


def rows_dot(left, right):
    return lax.dot_general(left, right, (((1,), (1,)), ((), ())), preferred_element_type=F32)


def plain_dot(left, right):
    return lax.dot_general(left, right, (((1,), (0,)), ((), ())), preferred_element_type=F32)


def own_rows(place, occ_fit, size):
    fit = occ_fit.shape[2]

    def body(place_ref, rows_ref, out_ref, sem):
        first = pl.multiple_of(place_ref[2] * size, 16)
        copy = pltpu.make_async_copy(rows_ref.at[0, pl.ds(first, size), :], out_ref, sem)
        copy.start()
        copy.wait()

    return pl.pallas_call(
        body,
        out_shape=jax.ShapeDtypeStruct((size, fit), BF),
        in_specs=[SMEM, pl.BlockSpec(memory_space=pl.ANY)],
        out_specs=VMEM,
        scratch_shapes=[pltpu.SemaphoreType.DMA],
        compiler_params=PARAMS,
        cost_estimate=pl.CostEstimate(flops=0, bytes_accessed=4 * size * fit, transcendentals=0),
    )(place, occ_fit)


def prepare(place, pair_block, block_rows, slab, slab_other):
    width, fit = slab.shape

    def body(place_ref, pair_ref, rows_ref, own_ref, other_ref, out_ref, mask_ref):
        out_ref[:, :width] = own_ref[...].T
        out_ref[:, width:] = other_ref[...].T
        me = place_ref[0]
        labels = rows_ref[pl.ds(place_ref[1], 1), :]
        first, second = labels[:, :width], labels[:, width:]
        swap = place_ref[2] == 1
        mine = jnp.where(swap, second, first)
        other = jnp.where(swap, first, second)
        for index, (dy, flip) in enumerate(PLACES):
            wanted = (pair_ref[me] + pair_ref[partner(me, dy, flip)]) & 1
            mask_ref[index : index + 1, :width] = jnp.where(mine == wanted, 1, 0)
            mask_ref[index : index + 1, width:] = jnp.where(other == wanted, 1, 0)

    return pl.pallas_call(
        body,
        out_shape=(
            jax.ShapeDtypeStruct((fit, 2 * width), BF),
            jax.ShapeDtypeStruct((len(PLACES), 2 * width), jnp.int32),
        ),
        in_specs=[SMEM, SMEM, VMEM, VMEM, VMEM],
        out_specs=(VMEM, VMEM),
        compiler_params=PARAMS,
        cost_estimate=pl.CostEstimate(
            flops=0, bytes_accessed=8 * fit * width, transcendentals=0
        ),
    )(place, pair_block, block_rows, slab, slab_other)


def fit_sums(place, parts, columns, scaled=False):
    count = len(parts)
    size = parts[0].shape[0]
    fit, width = columns.shape
    step = 2 * KEPT if size == 2 * KEPT else STRIDE
    shape = jax.ShapeDtypeStruct((count, KEPT, width), F32)
    if scaled:
        shapes = (jax.ShapeDtypeStruct((count * KEPT + FOOT, width), F32),)
    else:
        shapes = (shape, shape) if size == 2 * KEPT else (shape,)

    def body(place_ref, *refs):
        part_refs, columns_ref = refs[:count], refs[count]
        outs = refs[count + 1 : -2]
        stack_ref, total_ref = refs[-2:]
        for index in range(count):
            stack_ref[index * step : index * step + size, :] = part_refs[index][...]
        total_ref[...] = plain_dot(stack_ref[...], columns_ref[...])
        if size == 2 * KEPT:
            side = place_ref[3]
            for index in range(count):
                mine = pl.ds(pl.multiple_of(index * step + side * KEPT, 8), KEPT)
                other = pl.ds(pl.multiple_of(index * step + (1 - side) * KEPT, 8), KEPT)
                outs[0][index] = total_ref[mine, :]
                outs[1][index] = total_ref[other, :]
        elif not scaled:
            for index in range(count):
                outs[0][index] = total_ref[index * step : index * step + KEPT, :]
        else:
            blocks = [total_ref[index * step : index * step + KEPT, :] for index in range(count)]
            largest = jnp.max(jnp.abs(blocks[0]), axis=0, keepdims=True)
            for block in blocks[1:]:
                largest = jnp.maximum(largest, jnp.max(jnp.abs(block), axis=0, keepdims=True))
            largest = jnp.max(largest, axis=1, keepdims=True)
            exponent = jnp.floor(jnp.log2(jnp.maximum(largest, 1e-30)))
            scale = jnp.exp2(12.0 - exponent)
            for index in range(count):
                outs[0][index * KEPT : (index + 1) * KEPT, :] = blocks[index] * scale
            outs[0][count * KEPT :, :] = jnp.broadcast_to(exponent, (FOOT, width))

    return pl.pallas_call(
        body,
        out_shape=shapes,
        in_specs=[SMEM] + [VMEM] * (count + 1),
        out_specs=(VMEM,) * len(shapes),
        scratch_shapes=[pltpu.VMEM((count * step, fit), BF), pltpu.VMEM((count * step, width), F32)],
        compiler_params=PARAMS,
        cost_estimate=pl.CostEstimate(
            flops=2 * count * step * fit * width,
            bytes_accessed=2 * width * fit + 2 * count * size * fit + 8 * count * size * width,
            transcendentals=0,
        ),
    )(place, *parts, columns)


def apply_tile(place_ref, offset, block, own_ref, other_ref):
    width = own_ref.shape[1]
    own = other = None
    for index in range(2):
        row = (((place_ref[1] + offset) & (Z - 1)) * 2 + (place_ref[2] ^ index)) * width
        rows = pl.ds(pl.multiple_of(row, width), width)
        part = block[:, index * width : (index + 1) * width]
        to_own = plain_dot(part, own_ref[rows, :])
        to_other = plain_dot(part, other_ref[rows, :])
        own = to_own if own is None else own + to_own
        other = to_other if other is None else other + to_other
    return own, other


def apply_blocks(place, placed, fock, fock_other):
    offsets, blocks = zip(*placed)
    count = len(blocks)
    rows, columns = blocks[0].shape
    width = columns // 2

    def body(place_ref, *refs):
        own_ref, other_ref, out_ref = refs[count:]
        for index in range(count):
            own, other = apply_tile(
                place_ref, offsets[index], refs[index][...], own_ref, other_ref
            )
            if index == 0:
                out_ref[:, :width] = own
                out_ref[:, width:] = other
            else:
                out_ref[:, :width] += own
                out_ref[:, width:] += other

    return pl.pallas_call(
        body,
        out_shape=jax.ShapeDtypeStruct((rows, columns), F32),
        in_specs=[SMEM] + [VMEM] * (count + 2),
        out_specs=VMEM,
        compiler_params=PARAMS,
        cost_estimate=pl.CostEstimate(
            flops=2 * count * rows * columns * columns,
            bytes_accessed=2 * count * columns * (rows + columns),
            transcendentals=0,
        ),
    )(place, *blocks, fock, fock_other)


def contract(place, applied, placed, fock, fock_other, rights, pairs, mirrored):
    offsets, blocks = zip(*placed)
    rows, columns = blocks[0].shape
    width = columns // 2
    count = len(blocks)
    known = [] if applied is None else [applied]

    def body(place_ref, *refs):
        block_refs, (own_ref, other_ref) = refs[:count], refs[count : count + 2]
        known_refs = refs[count + 2 : count + 2 + len(known)]
        right_refs = refs[count + 2 + len(known) : count + 2 + len(known) + len(rights)]
        outs, sum_ref = refs[count + 2 + len(known) + len(rights) : -1], refs[-1]
        for index in range(count):
            own, other = apply_tile(
                place_ref, offsets[index], block_refs[index][...], own_ref, other_ref
            )
            if index == 0 and known:
                own += known_refs[0][:, :width]
                other += known_refs[0][:, width:]
            elif index > 0:
                own += sum_ref[:, :width]
                other += sum_ref[:, width:]
            sum_ref[:, :width] = own
            sum_ref[:, width:] = other
        pieces = [ref[index] for ref in right_refs for index in range(ref.shape[0])]
        sums = []
        for index, piece in enumerate(pieces):
            product = sum_ref[index * KEPT : (index + 1) * KEPT, :] * piece.astype(F32)
            sums.append(jnp.sum(jnp.sum(product, axis=0, keepdims=True), axis=1, keepdims=True))
        me = place_ref[0]
        lanes = lax.broadcasted_iota(jnp.int32, (1, OCC), 1)
        row = jnp.zeros((1, OCC), F32)
        for value, (dy, flip) in zip(sums, pairs):
            row += jnp.where(lanes == partner(me, dy, flip), value, 0.0)
        outs[0][...] = row
        for out, index in zip(outs[1:], mirrored):
            out[...] = jnp.where(lanes == me, sums[index], 0.0)

    shapes = (jax.ShapeDtypeStruct((1, OCC), F32),) * (1 + len(mirrored))
    return pl.pallas_call(
        body,
        out_shape=shapes,
        in_specs=[SMEM] + [VMEM] * (count + 2 + len(known) + len(rights)),
        out_specs=(VMEM,) * len(shapes),
        scratch_shapes=[pltpu.VMEM((rows, columns), F32)],
        compiler_params=PARAMS,
        cost_estimate=pl.CostEstimate(
            flops=2 * count * rows * columns * columns,
            bytes_accessed=2 * count * columns * (rows + columns) + 6 * rows * columns,
            transcendentals=0,
        ),
    )(place, *blocks, fock, fock_other, *known, *rights)


def shards(occ_fit, cabs_fit, fock, cabs_block, pair_block):
    me = lax.axis_index("occ")
    cabs = lax.axis_index("cabs")
    side = lax.axis_index("aux")
    core = cabs & 1
    z = cabs >> 1
    place = jnp.stack([me, z, core, side]).astype(jnp.int32)
    m_rows = occ_fit.shape[1]
    width = cabs_fit.shape[1]
    half = m_rows // 2

    own = own_rows(place, occ_fit, half)
    slab_other = core_swap(cabs_fit[0])
    fock_other = core_swap(fock)

    p0, a, b = occ_hop(own, 0, 1), occ_hop(own, 1, 0), occ_hop(own, -1, 0)
    columns, keep_column = prepare(
        place, pair_block, cabs_block.reshape(Z, 2 * width), cabs_fit[0], slab_other
    )
    p0, a, b, columns, fock_other = lax.optimization_barrier((p0, a, b, columns, fock_other))

    def head(value):
        return lax.dynamic_slice_in_dim(value, (1 - side) * KEPT, KEPT, 0)

    def tail(value):
        return lax.dynamic_slice_in_dim(value, side * KEPT, KEPT, 0)

    def second_round(p0, b):
        return occ_hop(b, 0, 1), occ_hop(p0, 1, 0), occ_hop(b, -1, 0), occ_hop(p0, 2, 0)

    heads = second_round(head(p0), head(b))
    tails = second_round(tail(p0), tail(b))

    def masked(keep, got, first):
        whole = (keep + got).astype(BF)
        mask = keep_column[first : first + keep.shape[0]]
        return jnp.where(mask[:, None] != 0, whole, jnp.zeros_like(whole))

    keep, send = fit_sums(place, [own, p0, a, b], columns)
    keep, *heads = lax.optimization_barrier((keep, *heads))
    got = aux_swap(send)
    got, *tails = lax.optimization_barrier((got, *tails))
    near = masked(keep, got, 0)
    (send,) = fit_sums(place, heads, columns, True)
    got = aux_swap(send.astype(jnp.float16))
    (keep,) = fit_sums(place, tails, columns)
    unscale = jnp.exp2(got[-1:].astype(F32) - 12.0)
    got = (got[:-FOOT].astype(F32) * unscale).reshape(keep.shape)
    far = masked(keep, got, 4)

    first = jnp.concatenate([near[1], near[2], far[1]], 0)
    second = jnp.concatenate([near[0], far[2], far[3]], 0)
    first_blocks, second_blocks = [(0, first)], [(0, second)]

    def ring_step(step, up, down, blocks):
        up, down = z_hop(up, 1), z_hop(down, -1)
        blocks.extend([(-step, up), (step, down)])
        return up, down

    rights = [jnp.stack([near[1], far[0], far[3]])]
    moves = [(0, 1), (1, 0), (2, 0)]
    up_a = down_a = first
    up_b = down_b = second
    for step in range(1, Z // 2):
        up_a, down_a, value = lax.optimization_barrier((up_a, down_a, rights[-1]))
        up_a, down_a = ring_step(step, up_a, down_a, first_blocks)
        value = occ_hop(value, *moves[step - 1])
        if step < Z // 2 - 1:
            up_a, down_a, value = lax.optimization_barrier((up_a, down_a, value))
        up_b, down_b = ring_step(step, up_b, down_b, second_blocks)
        rights[-1] = value
        if step == 1:
            rights.append(jnp.stack([near[3], value[1]]))
        elif step == 2:
            rights.append(jnp.stack([far[2], rights[0][2]]))
    first_blocks.append((Z // 2, z_hop(up_a, 1)))
    last_block = [(Z // 2, z_hop(down_b, -1))]
    row, to_a, to_pa = contract(
        place, None, first_blocks, fock, fock_other, [rights[0][:1], rights[1]], FIRST, (1, 2)
    )
    second = apply_blocks(place, second_blocks, fock, fock_other)
    (rest,) = contract(
        place, second, last_block, fock, fock_other, [near[:1], rights[2]], SECOND, ()
    )
    row += rest + occ_hop(to_a, -1, 0) + occ_hop(to_pa, -1, 1)
    peers = 4 * Z
    spread = lax.all_to_all(
        jnp.broadcast_to(row, (peers, OCC)), ("cabs", "aux"), 0, 0, tiled=True
    )
    return jnp.sum(spread, axis=0)[None, :]


def solution(mesh):
    in_specs = (P("occ", None, "aux"), P("occ", "cabs", "aux"), P(None, "cabs"), P(), P())
    out_specs = P("occ", None)
    return jax.shard_map(shards, mesh=mesh, in_specs=in_specs, out_specs=out_specs, check_vma=False)
```

```python
import jax
import jax.numpy as jnp
from jax import lax
from jax.experimental import pallas as pl
from jax.experimental.pallas import tpu as pltpu
from jax.sharding import PartitionSpec as P

BF = jnp.bfloat16
F32 = jnp.float32
Y = 4
Z = 8
OCC = 2 * Y
KEPT = 40
STRIDE = 48
FOOT = 16
VMEM = pl.BlockSpec(memory_space=pltpu.VMEM)
SMEM = pl.BlockSpec(memory_space=pltpu.SMEM)
PARAMS = pltpu.CompilerParams(vmem_limit_bytes=8 * 2**20)

PLACES = ((0, 0), (0, 1), (-1, 0), (1, 0), (1, 1), (-1, 1), (2, 0), (2, 1))
FIRST = ((0, 1), (-1, 0), (-1, 1))
SECOND = ((0, 0), (2, 0), (2, 1))


def partner(me, dy, flip):
    return (((me >> 1) + dy) & (Y - 1)) * 2 + ((me & 1) ^ flip)


def occ_hop(value, dy, flip):
    return lax.ppermute(value, "occ", [(o, partner(o, dy, flip)) for o in range(OCC)])


def z_hop(value, dz):
    return lax.ppermute(value, "cabs", [(c, ((c // 2 + dz) % Z) * 2 + c % 2) for c in range(2 * Z)])


def core_swap(value):
    return lax.ppermute(value, "cabs", [(c, c ^ 1) for c in range(2 * Z)])


def aux_swap(value):
    return lax.ppermute(value, "aux", [(0, 1), (1, 0)])


def rows_dot(left, right):
    return lax.dot_general(left, right, (((1,), (1,)), ((), ())), preferred_element_type=F32)


def plain_dot(left, right):
    return lax.dot_general(left, right, (((1,), (0,)), ((), ())), preferred_element_type=F32)


def own_rows(place, occ_fit, size):
    fit = occ_fit.shape[2]

    def body(place_ref, rows_ref, out_ref, sem):
        first = pl.multiple_of(place_ref[2] * size, 16)
        copy = pltpu.make_async_copy(rows_ref.at[0, pl.ds(first, size), :], out_ref, sem)
        copy.start()
        copy.wait()

    return pl.pallas_call(
        body,
        out_shape=jax.ShapeDtypeStruct((size, fit), BF),
        in_specs=[SMEM, pl.BlockSpec(memory_space=pl.ANY)],
        out_specs=VMEM,
        scratch_shapes=[pltpu.SemaphoreType.DMA],
        compiler_params=PARAMS,
        cost_estimate=pl.CostEstimate(flops=0, bytes_accessed=4 * size * fit, transcendentals=0),
    )(place, occ_fit)


def prepare(place, pair_block, block_rows, slab, slab_other):
    width, fit = slab.shape

    def body(place_ref, pair_ref, rows_ref, own_ref, other_ref, out_ref, mask_ref):
        out_ref[:, :width] = own_ref[...].T
        out_ref[:, width:] = other_ref[...].T
        me = place_ref[0]
        labels = rows_ref[pl.ds(place_ref[1], 1), :]
        first, second = labels[:, :width], labels[:, width:]
        swap = place_ref[2] == 1
        mine = jnp.where(swap, second, first)
        other = jnp.where(swap, first, second)
        for index, (dy, flip) in enumerate(PLACES):
            wanted = (pair_ref[me] + pair_ref[partner(me, dy, flip)]) & 1
            mask_ref[index : index + 1, :width] = jnp.where(mine == wanted, 1, 0)
            mask_ref[index : index + 1, width:] = jnp.where(other == wanted, 1, 0)

    return pl.pallas_call(
        body,
        out_shape=(
            jax.ShapeDtypeStruct((fit, 2 * width), BF),
            jax.ShapeDtypeStruct((len(PLACES), 2 * width), jnp.int32),
        ),
        in_specs=[SMEM, SMEM, VMEM, VMEM, VMEM],
        out_specs=(VMEM, VMEM),
        compiler_params=PARAMS,
        cost_estimate=pl.CostEstimate(
            flops=0, bytes_accessed=8 * fit * width, transcendentals=0
        ),
    )(place, pair_block, block_rows, slab, slab_other)


def fit_sums(place, parts, columns, scaled=False):
    count = len(parts)
    size = parts[0].shape[0]
    fit, width = columns.shape
    step = 2 * KEPT if size == 2 * KEPT else STRIDE
    shape = jax.ShapeDtypeStruct((count, KEPT, width), F32)
    if scaled:
        shapes = (jax.ShapeDtypeStruct((count * KEPT + FOOT, width), F32),)
    else:
        shapes = (shape, shape) if size == 2 * KEPT else (shape,)

    def body(place_ref, *refs):
        part_refs, columns_ref = refs[:count], refs[count]
        outs = refs[count + 1 : -2]
        stack_ref, total_ref = refs[-2:]
        for index in range(count):
            stack_ref[index * step : index * step + size, :] = part_refs[index][...]
        total_ref[...] = plain_dot(stack_ref[...], columns_ref[...])
        if size == 2 * KEPT:
            side = place_ref[3]
            for index in range(count):
                mine = pl.ds(pl.multiple_of(index * step + side * KEPT, 8), KEPT)
                other = pl.ds(pl.multiple_of(index * step + (1 - side) * KEPT, 8), KEPT)
                outs[0][index] = total_ref[mine, :]
                outs[1][index] = total_ref[other, :]
        elif not scaled:
            for index in range(count):
                outs[0][index] = total_ref[index * step : index * step + KEPT, :]
        else:
            blocks = [total_ref[index * step : index * step + KEPT, :] for index in range(count)]
            largest = jnp.max(jnp.abs(blocks[0]), axis=0, keepdims=True)
            for block in blocks[1:]:
                largest = jnp.maximum(largest, jnp.max(jnp.abs(block), axis=0, keepdims=True))
            largest = jnp.max(largest, axis=1, keepdims=True)
            exponent = jnp.floor(jnp.log2(jnp.maximum(largest, 1e-30)))
            scale = jnp.exp2(12.0 - exponent)
            for index in range(count):
                outs[0][index * KEPT : (index + 1) * KEPT, :] = blocks[index] * scale
            outs[0][count * KEPT :, :] = jnp.broadcast_to(exponent, (FOOT, width))

    return pl.pallas_call(
        body,
        out_shape=shapes,
        in_specs=[SMEM] + [VMEM] * (count + 1),
        out_specs=(VMEM,) * len(shapes),
        scratch_shapes=[pltpu.VMEM((count * step, fit), BF), pltpu.VMEM((count * step, width), F32)],
        compiler_params=PARAMS,
        cost_estimate=pl.CostEstimate(
            flops=2 * count * step * fit * width,
            bytes_accessed=2 * width * fit + 2 * count * size * fit + 8 * count * size * width,
            transcendentals=0,
        ),
    )(place, *parts, columns)


def apply_tile(place_ref, offset, block, own_ref, other_ref):
    width = own_ref.shape[1]
    own = other = None
    for index in range(2):
        row = (((place_ref[1] + offset) & (Z - 1)) * 2 + (place_ref[2] ^ index)) * width
        rows = pl.ds(pl.multiple_of(row, width), width)
        part = block[:, index * width : (index + 1) * width]
        to_own = plain_dot(part, own_ref[rows, :])
        to_other = plain_dot(part, other_ref[rows, :])
        own = to_own if own is None else own + to_own
        other = to_other if other is None else other + to_other
    return own, other


def apply_blocks(place, placed, fock, fock_other):
    offsets, blocks = zip(*placed)
    count = len(blocks)
    rows, columns = blocks[0].shape
    width = columns // 2

    def body(place_ref, *refs):
        own_ref, other_ref, out_ref = refs[count:]
        for index in range(count):
            own, other = apply_tile(
                place_ref, offsets[index], refs[index][...], own_ref, other_ref
            )
            if index == 0:
                out_ref[:, :width] = own
                out_ref[:, width:] = other
            else:
                out_ref[:, :width] += own
                out_ref[:, width:] += other

    return pl.pallas_call(
        body,
        out_shape=jax.ShapeDtypeStruct((rows, columns), F32),
        in_specs=[SMEM] + [VMEM] * (count + 2),
        out_specs=VMEM,
        compiler_params=PARAMS,
        cost_estimate=pl.CostEstimate(
            flops=2 * count * rows * columns * columns,
            bytes_accessed=2 * count * columns * (rows + columns),
            transcendentals=0,
        ),
    )(place, *blocks, fock, fock_other)


def contract(place, applied, placed, fock, fock_other, rights, pairs, mirrored):
    offsets, blocks = zip(*placed)
    rows, columns = blocks[0].shape
    width = columns // 2
    count = len(blocks)
    known = [] if applied is None else [applied]

    def body(place_ref, *refs):
        block_refs, (own_ref, other_ref) = refs[:count], refs[count : count + 2]
        known_refs = refs[count + 2 : count + 2 + len(known)]
        right_refs = refs[count + 2 + len(known) : count + 2 + len(known) + len(rights)]
        outs, sum_ref = refs[count + 2 + len(known) + len(rights) : -1], refs[-1]
        for index in range(count):
            own, other = apply_tile(
                place_ref, offsets[index], block_refs[index][...], own_ref, other_ref
            )
            if index == 0 and known:
                own += known_refs[0][:, :width]
                other += known_refs[0][:, width:]
            elif index > 0:
                own += sum_ref[:, :width]
                other += sum_ref[:, width:]
            sum_ref[:, :width] = own
            sum_ref[:, width:] = other
        pieces = [ref[index] for ref in right_refs for index in range(ref.shape[0])]
        sums = []
        for index, piece in enumerate(pieces):
            product = sum_ref[index * KEPT : (index + 1) * KEPT, :] * piece.astype(F32)
            sums.append(jnp.sum(jnp.sum(product, axis=0, keepdims=True), axis=1, keepdims=True))
        me = place_ref[0]
        lanes = lax.broadcasted_iota(jnp.int32, (1, OCC), 1)
        row = jnp.zeros((1, OCC), F32)
        for value, (dy, flip) in zip(sums, pairs):
            row += jnp.where(lanes == partner(me, dy, flip), value, 0.0)
        outs[0][...] = row
        for out, index in zip(outs[1:], mirrored):
            out[...] = jnp.where(lanes == me, sums[index], 0.0)

    shapes = (jax.ShapeDtypeStruct((1, OCC), F32),) * (1 + len(mirrored))
    return pl.pallas_call(
        body,
        out_shape=shapes,
        in_specs=[SMEM] + [VMEM] * (count + 2 + len(known) + len(rights)),
        out_specs=(VMEM,) * len(shapes),
        scratch_shapes=[pltpu.VMEM((rows, columns), F32)],
        compiler_params=PARAMS,
        cost_estimate=pl.CostEstimate(
            flops=2 * count * rows * columns * columns,
            bytes_accessed=2 * count * columns * (rows + columns) + 6 * rows * columns,
            transcendentals=0,
        ),
    )(place, *blocks, fock, fock_other, *known, *rights)


def shards(occ_fit, cabs_fit, fock, cabs_block, pair_block):
    me = lax.axis_index("occ")
    cabs = lax.axis_index("cabs")
    side = lax.axis_index("aux")
    core = cabs & 1
    z = cabs >> 1
    place = jnp.stack([me, z, core, side]).astype(jnp.int32)
    m_rows = occ_fit.shape[1]
    width = cabs_fit.shape[1]
    half = m_rows // 2

    own = own_rows(place, occ_fit, half)
    slab_other = core_swap(cabs_fit[0])
    fock_other = core_swap(fock)

    p0, a, b = occ_hop(own, 0, 1), occ_hop(own, 1, 0), occ_hop(own, -1, 0)
    columns, keep_column = prepare(
        place, pair_block, cabs_block.reshape(Z, 2 * width), cabs_fit[0], slab_other
    )
    p0, a, b, columns, fock_other = lax.optimization_barrier((p0, a, b, columns, fock_other))

    def head(value):
        return lax.dynamic_slice_in_dim(value, (1 - side) * KEPT, KEPT, 0)

    def tail(value):
        return lax.dynamic_slice_in_dim(value, side * KEPT, KEPT, 0)

    def second_round(p0, b):
        return occ_hop(b, 0, 1), occ_hop(p0, 1, 0), occ_hop(b, -1, 0), occ_hop(p0, 2, 0)

    heads = second_round(head(p0), head(b))
    tails = second_round(tail(p0), tail(b))

    def masked(keep, got, first):
        whole = (keep + got).astype(BF)
        mask = keep_column[first : first + keep.shape[0]]
        return jnp.where(mask[:, None] != 0, whole, jnp.zeros_like(whole))

    keep, send = fit_sums(place, [own, p0, a, b], columns)
    keep, *heads = lax.optimization_barrier((keep, *heads))
    got = aux_swap(send)
    got, *tails = lax.optimization_barrier((got, *tails))
    near = masked(keep, got, 0)
    (send,) = fit_sums(place, heads, columns, True)
    got = aux_swap(send.astype(jnp.float16))
    (keep,) = fit_sums(place, tails, columns)
    unscale = jnp.exp2(got[-1:].astype(F32) - 12.0)
    got = (got[:-FOOT].astype(F32) * unscale).reshape(keep.shape)
    far = masked(keep, got, 4)

    first = jnp.concatenate([near[1], near[2], far[1]], 0)
    second = jnp.concatenate([near[0], far[2], far[3]], 0)
    first_blocks, second_blocks = [(0, first)], [(0, second)]

    def ring_step(step, up, down, blocks):
        up, down = z_hop(up, 1), z_hop(down, -1)
        blocks.extend([(-step, up), (step, down)])
        return up, down

    rights = [jnp.stack([near[1], far[0], far[3]])]
    moves = [(0, 1), (1, 0), (2, 0)]
    up_a = down_a = first
    up_b = down_b = second
    for step in range(1, Z // 2):
        up_a, down_a, value = lax.optimization_barrier((up_a, down_a, rights[-1]))
        up_a, down_a = ring_step(step, up_a, down_a, first_blocks)
        value = occ_hop(value, *moves[step - 1])
        up_b, down_b = ring_step(step, up_b, down_b, second_blocks)
        if step < Z // 2 - 1:
            up_b, down_b, value = lax.optimization_barrier((up_b, down_b, value))
        rights[-1] = value
        if step == 1:
            rights.append(jnp.stack([near[3], value[1]]))
        elif step == 2:
            rights.append(jnp.stack([far[2], rights[0][2]]))
    first_blocks.append((Z // 2, z_hop(up_a, 1)))
    last_block = [(Z // 2, z_hop(down_b, -1))]
    row, to_a, to_pa = contract(
        place, None, first_blocks, fock, fock_other, [rights[0][:1], rights[1]], FIRST, (1, 2)
    )
    second = apply_blocks(place, second_blocks, fock, fock_other)
    (rest,) = contract(
        place, second, last_block, fock, fock_other, [near[:1], rights[2]], SECOND, ()
    )
    row += rest + occ_hop(to_a, -1, 0) + occ_hop(to_pa, -1, 1)
    peers = 4 * Z
    spread = lax.all_to_all(
        jnp.broadcast_to(row, (peers, OCC)), ("cabs", "aux"), 0, 0, tiled=True
    )
    return jnp.sum(spread, axis=0)[None, :]


def solution(mesh):
    in_specs = (P("occ", None, "aux"), P("occ", "cabs", "aux"), P(None, "cabs"), P(), P())
    out_specs = P("occ", None)
    return jax.shard_map(shards, mesh=mesh, in_specs=in_specs, out_specs=out_specs, check_vma=False)
```
